32 devices in a mesh: col: 4 (over z), depth: 8 (over y, x, core).
Axes of the slice: x: 2, y: 2, z: 4, core: 2. Of those that a mesh axis runs over, the one named last changes fastest.
Arguments:
- volume: bfloat16 [128, 256, 512], P('depth', None, 'col'), may hold values from -6 to 6
- tf_index: int32 [128, 256, 512], P('depth', None, 'col'), may hold values from 0 to 255
- tf_table: bfloat16 [4, 256], replicated, may hold values from 0 to 1, as said below
Outputs:
- frame: float32 [4, 256, 512], P(None, 'depth', 'col')
The draws below stay inside these ranges and needn't reach their ends.
Inputs may be any that keep to these rules, and one draw needn't show every extreme that they name: Rows 0 to 2 of tf_table are positive colours; row 3 is a positive extinction.
All inputs are finite; a program needn't handle non-finite values.
Results may differ from the reference program's by a relative error of at most 0.005.
Values may be sent and summed in bfloat16 or wider, within the bound.
A program may use at most 128 MiB of HBM per device.

```python
import math
import jax
import jax.numpy as jnp
from jax import lax

CY = 256
TABLE_ENTRIES = 256
NX = 512
NZ = 128


def draw_tf_table(key, part):
    color_random_key, extinction_random_key, threshold_random_key, surge_random_key = jax.random.split(key, 4)
    color_lo, color_hi, sigma_lo, sigma_hi = (0.2, 1.0, 0.2 / NZ, 4.0 / NZ)
    colors = jax.random.uniform(color_random_key, (3, TABLE_ENTRIES), jnp.float32, color_lo, color_hi)
    logs = jax.random.uniform(extinction_random_key, (TABLE_ENTRIES,), jnp.float32, math.log(sigma_lo), math.log(sigma_hi))
    extinction_coefficient = jnp.exp(logs)
    surge_threshold = jax.random.randint(threshold_random_key, (), 0, TABLE_ENTRIES)
    emission_surge = jax.random.uniform(surge_random_key, (), jnp.float32, 0.25, 0.5)
    extinction_coefficient = jnp.where(jnp.arange(TABLE_ENTRIES) == surge_threshold, emission_surge, extinction_coefficient)
    return jnp.concatenate([colors, extinction_coefficient[None]], 0).astype(jnp.bfloat16)


def set_ends(drawn, stream_key, smallest, largest):
    extent = drawn.shape
    index_at = [jax.random.randint(jax.random.fold_in(stream_key, axis), (), 0, extent[axis]) for axis in range(len(extent))]
    drawn = drawn.at[tuple(index_at)].set(smallest)
    longest = extent.index(max(extent))
    index_at[longest] = (index_at[longest] + 1) % extent[longest]
    return drawn.at[tuple(index_at)].set(largest)


def level_of(stream_key, extent, cuts, low, largest):
    factor_of = 1.0
    for position, parts in cuts:
        heights = jax.random.uniform(jax.random.fold_in(jax.random.fold_in(stream_key, 6), position), (parts,), jnp.float32, low / len(cuts), largest / len(cuts))
        factor_of = factor_of * jnp.repeat(jnp.exp(heights), extent[position] // parts).reshape((-1,) + (1,) * (len(extent) - 1 - position))
    return factor_of


def scatter_about(rng, shape, deviation, bound, shards=(), held_as=jnp.bfloat16):
    array = jax.random.normal(rng, shape, jnp.float32) * deviation
    if len(shards) > 0:
        array = level_of(rng, shape, shards, -0.22, 0.18) * array
    return jnp.clip(array, min=-bound, max=bound).astype(held_as)


def setup_inputs(seed: int = 0) -> dict:
    streams_of = jax.random.split(jax.random.key(seed), 4)
    return {
        "volume": scatter_about(streams_of[0], (NZ, CY, NX), 1.0, 6.0, ((0, 8), (2, 4))),
        "tf_index": set_ends(jax.random.randint(streams_of[1], (NZ, CY, NX), 0, TABLE_ENTRIES), jax.random.fold_in(streams_of[1], 1), 0, TABLE_ENTRIES - 1).astype(jnp.int32),
        "tf_table": draw_tf_table(jax.random.fold_in(streams_of[3], 71), 0),
    }


light_across = 0.36
light_down = 0.48
light_depth = 0.8

def shading(grad_x, grad_y, grad_z):
    facing = grad_x * light_across + grad_y * light_down + grad_z * light_depth
    return 0.25 + 0.75 * jnp.abs(facing) / jnp.sqrt(grad_x * grad_x + grad_y * grad_y + grad_z * grad_z + 1.0)

def reference(volume, tf_index, tf_table):
    padded = jnp.pad(volume, ((1, 1), (1, 1), (1, 1)))
    table = tf_table.astype(jnp.float32)

    def march(carry, depth_pos):
        color_sum, optical = carry
        above = lax.dynamic_index_in_dim(padded, depth_pos, 0, keepdims=False).astype(jnp.float32)
        middle = lax.dynamic_index_in_dim(padded, depth_pos + 1, 0, keepdims=False).astype(jnp.float32)
        below = lax.dynamic_index_in_dim(padded, depth_pos + 2, 0, keepdims=False).astype(jnp.float32)
        grad_x = (middle[1:-1, 2:] - middle[1:-1, :-2]) * 0.5
        grad_y = (middle[2:, 1:-1] - middle[:-2, 1:-1]) * 0.5
        grad_z = (below[1:-1, 1:-1] - above[1:-1, 1:-1]) * 0.5
        shade = shading(grad_x, grad_y, grad_z)
        levels = lax.dynamic_index_in_dim(tf_index, depth_pos, 0, keepdims=False)
        looked = table[:, levels]
        extinction_coefficient = looked[3]
        alpha = -jnp.expm1(-extinction_coefficient)
        weight = jnp.exp(-optical) * alpha * shade
        color_sum = color_sum + weight[None] * looked[:3]
        return ((color_sum, optical + extinction_coefficient), None)
    start = (jnp.zeros((3, CY, NX), jnp.float32), jnp.zeros((CY, NX), jnp.float32))
    (color_sum, optical), _ = lax.scan(march, start, jnp.arange(NZ, dtype=jnp.int32))
    return jnp.concatenate([color_sum, (-jnp.expm1(-optical))[None]], 0)
```

```python
import functools

import jax
import jax.numpy as jnp
from jax import lax
from jax.experimental import pallas as pl
from jax.experimental.pallas import tpu as pltpu
from jax.sharding import PartitionSpec as P

LIGHT = (0.75 * 0.36, 0.75 * 0.48, 0.75 * 0.8)
LOG2E = 1.4426950408889634
LN2 = 0.6931471805599453
PAD = 8


def one_minus_exp(x):
    series = x * (1.0 - x * (0.5 - x * (1.0 / 6.0 - x * (1.0 / 24.0 - x * (1.0 / 120.0)))))
    return jnp.where(x < 0.125, series, 1.0 - jnp.exp(-x))


def kernel(n, vol, idx, table, zlo, zhi, hx, out, fvol, dx, part, recv, send_sem, recv_sem):
    depth, rows, cols = vol.shape
    rb = rows // n
    me = lax.axis_index("depth")

    barrier = pltpu.get_barrier_semaphore()

    def greet(k, c):
        pl.semaphore_signal(barrier, inc=1, device_id={"depth": lax.rem(me + 1 + k, n)},
                            device_id_type=pl.DeviceIdType.MESH)
        return c

    lax.fori_loop(0, n - 1, greet, 0)

    r_i = lax.broadcasted_iota(jnp.int32, (cols, cols), 0)
    c_i = lax.broadcasted_iota(jnp.int32, (cols, cols), 1)
    diff = jnp.where(r_i == c_i + 1, 1.0, 0.0) - jnp.where(r_i == c_i - 1, 1.0, 0.0)
    diff = diff.astype(jnp.bfloat16)
    zero = jnp.zeros((PAD, cols), jnp.float32)
    halo = hx[...]

    def stage(z, c):
        v = vol[z]
        fvol[z + 1, :PAD] = zero
        fvol[z + 1, PAD + rows:] = zero
        fvol[z + 1, PAD:PAD + rows] = v.astype(jnp.float32)
        edge = jnp.where((c_i == cols - 1) & (r_i == depth + z), 1.0, 0.0)
        edge = edge - jnp.where((c_i == 0) & (r_i == z), 1.0, 0.0)
        weights = jnp.concatenate([diff, edge.astype(jnp.bfloat16)], 0)
        both = jnp.concatenate([v, halo], 1)
        dx[z] = jnp.dot(both, weights, preferred_element_type=jnp.float32)
        return c

    lax.fori_loop(0, depth, stage, 0)
    fvol[0, PAD:PAD + rows] = zlo[...].astype(jnp.float32)
    fvol[depth + 1, PAD:PAD + rows] = zhi[...].astype(jnp.float32)

    entries = table[...].astype(jnp.float32)
    sigma = entries[3:4]
    alpha = one_minus_exp(sigma)
    tables = [entries[c:c + 1] * alpha for c in range(3)] + [sigma * -LOG2E]
    sub = 8
    low = [jnp.broadcast_to(t[:, :128], (sub, 128)) for t in tables]
    high = [jnp.broadcast_to(t[:, 128:], (sub, 128)) for t in tables]

    def block(r0):
        def step(z, carry):
            acc0, acc1, acc2, s = carry
            at = pl.multiple_of(PAD + r0, 8)
            gx = dx[z, pl.ds(pl.multiple_of(r0, 8), sub)]
            gy = fvol[z + 1, pl.ds(at + 1, sub)] - fvol[z + 1, pl.ds(at - 1, sub)]
            gz = fvol[z + 2, pl.ds(at, sub)] - fvol[z, pl.ds(at, sub)]
            facing = gx * LIGHT[0] + gy * LIGHT[1] + gz * LIGHT[2]
            inv = lax.rsqrt(gx * gx + gy * gy + (gz * gz + 4.0))
            shade = 0.25 + jnp.abs(facing) * inv
            label = idx[z, pl.ds(pl.multiple_of(r0, 8), sub)]
            in_low = label < 128
            lane = label & 127
            look = [jnp.where(in_low, jnp.take_along_axis(lo, lane, axis=1),
                              jnp.take_along_axis(hi, lane, axis=1))
                    for lo, hi in zip(low, high)]
            w = jnp.exp2(s) * shade
            return (acc0 + w * look[0], acc1 + w * look[1], acc2 + w * look[2], s + look[3])

        init = tuple(jnp.zeros((sub, cols), jnp.float32) for _ in range(4))
        return lax.fori_loop(0, depth, step, init, unroll=True)

    def compute(d):
        tiles = [block(d * rb + sub * i) for i in range(rb // sub)]
        return jnp.concatenate([t[c] for c in range(4) for t in tiles], 0).astype(jnp.bfloat16)

    def copy(k):
        return pltpu.make_async_remote_copy(
            src_ref=part.at[k], dst_ref=recv.at[k],
            send_sem=send_sem.at[k], recv_sem=recv_sem.at[k],
            device_id={"depth": lax.rem(me + 1 + k, n)},
            device_id_type=pl.DeviceIdType.MESH)

    pl.semaphore_wait(barrier, n - 1)

    def work(k, c):
        part[k] = compute(lax.rem(me + 1 + k, n))
        copy(k).start()
        return c

    lax.fori_loop(0, n - 1, work, 0)
    recv[n - 1] = compute(me)

    def arrive(k, c):
        copy(k).wait()
        return c

    lax.fori_loop(0, n - 1, arrive, 0)

    def over(j, carry):
        color, s = carry
        piece = recv[lax.rem(me - j - 1 + 2 * n, n)].astype(jnp.float32)
        t = jnp.exp2(s)
        color = tuple(color[c] + t * piece[c * rb:(c + 1) * rb] for c in range(3))
        return color, s + piece[3 * rb:]

    init = jnp.zeros((rb, cols), jnp.float32)
    color, s = lax.fori_loop(0, n, over, ((init,) * 3, init))
    for c in range(3):
        out[c] = color[c]
    out[3] = one_minus_exp(s * -LN2)


def on_device(volume, tf_index, tf_table):
    depth, rows, cols = volume.shape
    n = lax.axis_size("depth")
    across = lax.axis_size("col")
    up = lambda m: [(i, i + 1) for i in range(m - 1)]
    down = lambda m: [(i + 1, i) for i in range(m - 1)]
    zlo = lax.ppermute(volume[-1], "depth", up(n))
    zhi = lax.ppermute(volume[0], "depth", down(n))
    left = lax.ppermute(volume[:, :, -1], "col", up(across))
    right = lax.ppermute(volume[:, :, 0], "col", down(across))
    hx = jnp.concatenate([left, right], 0).T
    hx = jnp.pad(hx, ((0, 0), (0, cols - 2 * depth)))
    vm = pl.BlockSpec(memory_space=pltpu.VMEM)
    rb = rows // n
    return pl.pallas_call(
        functools.partial(kernel, n),
        out_shape=jax.ShapeDtypeStruct((4, rb, cols), jnp.float32),
        in_specs=[vm] * 6,
        out_specs=vm,
        scratch_shapes=[
            pltpu.VMEM((depth + 2, rows + 2 * PAD, cols), jnp.float32),
            pltpu.VMEM((depth, rows, cols), jnp.float32),
            pltpu.VMEM((n, 4 * rb, cols), jnp.bfloat16),
            pltpu.VMEM((n, 4 * rb, cols), jnp.bfloat16),
            pltpu.SemaphoreType.DMA((n - 1,)),
            pltpu.SemaphoreType.DMA((n - 1,)),
        ],
        compiler_params=pltpu.CompilerParams(
            collective_id=0, has_side_effects=True, vmem_limit_bytes=32 * 1024 * 1024),
    )(volume, tf_index, tf_table, zlo, zhi, hx)


def solution(mesh):
    in_specs = (P("depth", None, "col"), P("depth", None, "col"), P())
    out_specs = P(None, "depth", "col")
    return jax.shard_map(
        on_device, mesh=mesh, in_specs=in_specs, out_specs=out_specs, check_vma=False
    )
```

```python
import functools

import jax
import jax.numpy as jnp
from jax import lax
from jax.experimental import pallas as pl
from jax.experimental.pallas import tpu as pltpu
from jax.sharding import PartitionSpec as P

LIGHT = (0.75 * 0.36, 0.75 * 0.48, 0.75 * 0.8)
LOG2E = 1.4426950408889634
LN2 = 0.6931471805599453
PAD = 8


def one_minus_exp(x):
    series = x * (1.0 - x * (0.5 - x * (1.0 / 6.0 - x * (1.0 / 24.0 - x * (1.0 / 120.0)))))
    return jnp.where(x < 0.125, series, 1.0 - jnp.exp(-x))


def kernel(n, m, vol, idx, table, out, fvol, dx, part, recv, edge, zlo, zhi, from_left, from_right,
           send_sem, recv_sem, halo_send, halo_recv):
    depth, rows, cols = vol.shape
    rb = rows // n
    me = lax.axis_index("depth")
    mine = lax.axis_index("col")

    barrier = pltpu.get_barrier_semaphore()

    def greet(k, c):
        pl.semaphore_signal(barrier, inc=1, device_id={"depth": lax.rem(me + 1 + k, n)},
                            device_id_type=pl.DeviceIdType.MESH)
        return c

    lax.fori_loop(0, n - 1, greet, 0)
    for there, side in ((mine > 0, -1), (mine < m - 1, 1)):
        @pl.when(there)
        def _():
            pl.semaphore_signal(barrier, inc=1, device_id={"col": mine + side},
                                device_id_type=pl.DeviceIdType.MESH)

    def halo_copy(k, src, dst, axis, to):
        return pltpu.make_async_remote_copy(
            src_ref=src, dst_ref=dst, send_sem=halo_send.at[k], recv_sem=halo_recv.at[k],
            device_id={axis: to}, device_id_type=pl.DeviceIdType.MESH)

    along_z = ((me > 0, me < n - 1, halo_copy(0, vol.at[0], zhi, "depth", me - 1), zhi),
               (me < n - 1, me > 0, halo_copy(1, vol.at[depth - 1], zlo, "depth", me + 1), zlo))
    along_x = ((mine > 0, mine < m - 1, halo_copy(2, edge, from_right, "col", mine - 1), from_right),
               (mine < m - 1, mine > 0, halo_copy(3, edge, from_left, "col", mine + 1), from_left))

    def send(halos):
        for sends, _, copy, _ in halos:
            pl.when(sends)(copy.start)

    def receive(halos):
        for sends, receives, copy, landed in halos:
            pl.when(sends)(copy.wait_send)
            pl.when(receives)(copy.wait_recv)

            @pl.when(jnp.logical_not(receives))
            def _():
                landed[...] = jnp.zeros_like(landed)

    neighbours = (mine > 0).astype(jnp.int32) + (mine < m - 1).astype(jnp.int32)
    pl.semaphore_wait(barrier, n - 1 + neighbours)
    send(along_z)

    r_i = lax.broadcasted_iota(jnp.int32, (cols, cols), 0)
    c_i = lax.broadcasted_iota(jnp.int32, (cols, cols), 1)
    diff = jnp.where(r_i == c_i + 1, 1.0, 0.0) - jnp.where(r_i == c_i - 1, 1.0, 0.0)
    diff = diff.astype(jnp.bfloat16)
    zero = jnp.zeros((PAD, cols), jnp.float32)

    def pick(z, total):
        at = jnp.where((r_i == cols - 1) & (c_i == z), 1.0, 0.0)
        at = at + jnp.where((r_i == 0) & (c_i == depth + z), 1.0, 0.0)
        return total + jnp.dot(vol[z], at.astype(jnp.bfloat16), preferred_element_type=jnp.float32)

    edges = lax.fori_loop(0, depth, pick, jnp.zeros((rows, cols), jnp.float32), unroll=4)
    edge[...] = edges.astype(jnp.bfloat16)
    send(along_x)

    def widen(z, c):
        v = vol[z]
        fvol[z + 1, :PAD] = zero
        fvol[z + 1, PAD + rows:] = zero
        fvol[z + 1, PAD:PAD + rows] = v.astype(jnp.float32)
        return c

    lax.fori_loop(0, depth, widen, 0, unroll=2)
    receive(along_x)
    lane = lax.broadcasted_iota(jnp.int32, (rows, cols), 1)
    halo = jnp.where(lane < depth, from_left[...].astype(jnp.float32), from_right[...].astype(jnp.float32))
    halo = halo.astype(jnp.bfloat16)

    def stage(z, c):
        v = vol[z]
        ends = jnp.where((c_i == cols - 1) & (r_i == depth + z), 1.0, 0.0)
        ends = ends - jnp.where((c_i == 0) & (r_i == z), 1.0, 0.0)
        weights = jnp.concatenate([diff, ends.astype(jnp.bfloat16)], 0)
        both = jnp.concatenate([v, halo], 1)
        dx[z] = jnp.dot(both, weights, preferred_element_type=jnp.float32)
        return c

    lax.fori_loop(0, depth, stage, 0, unroll=4)
    receive(along_z)
    fvol[0, PAD:PAD + rows] = zlo[...].astype(jnp.float32)
    fvol[depth + 1, PAD:PAD + rows] = zhi[...].astype(jnp.float32)

    entries = table[...].astype(jnp.float32)
    sigma = entries[3:4]
    alpha = one_minus_exp(sigma)
    tables = [entries[c:c + 1] * alpha for c in range(3)] + [sigma * -LOG2E]
    sub = 8
    low = [jnp.broadcast_to(t[:, :128], (sub, 128)) for t in tables]
    high = [jnp.broadcast_to(t[:, 128:], (sub, 128)) for t in tables]

    def block(r0):
        def step(z, carry):
            acc0, acc1, acc2, s = carry
            at = pl.multiple_of(PAD + r0, 8)
            gx = dx[z, pl.ds(pl.multiple_of(r0, 8), sub)]
            gy = fvol[z + 1, pl.ds(at + 1, sub)] - fvol[z + 1, pl.ds(at - 1, sub)]
            gz = fvol[z + 2, pl.ds(at, sub)] - fvol[z, pl.ds(at, sub)]
            facing = gx * LIGHT[0] + gy * LIGHT[1] + gz * LIGHT[2]
            inv = lax.rsqrt(gx * gx + gy * gy + (gz * gz + 4.0))
            shade = 0.25 + jnp.abs(facing) * inv
            label = idx[z, pl.ds(pl.multiple_of(r0, 8), sub)]
            in_low = label < 128
            lane = label & 127
            look = [jnp.where(in_low, jnp.take_along_axis(lo, lane, axis=1),
                              jnp.take_along_axis(hi, lane, axis=1))
                    for lo, hi in zip(low, high)]
            w = jnp.exp2(s) * shade
            return (acc0 + w * look[0], acc1 + w * look[1], acc2 + w * look[2], s + look[3])

        init = tuple(jnp.zeros((sub, cols), jnp.float32) for _ in range(4))
        return lax.fori_loop(0, depth, step, init, unroll=True)

    def compute(d):
        tiles = [block(d * rb + sub * i) for i in range(rb // sub)]
        return jnp.concatenate([t[c] for c in range(4) for t in tiles], 0).astype(jnp.bfloat16)

    def copy(k):
        return pltpu.make_async_remote_copy(
            src_ref=part.at[k], dst_ref=recv.at[k],
            send_sem=send_sem.at[k], recv_sem=recv_sem.at[k],
            device_id={"depth": lax.rem(me + 1 + k, n)},
            device_id_type=pl.DeviceIdType.MESH)

    def work(k, c):
        part[k] = compute(lax.rem(me + 1 + k, n))
        copy(k).start()
        return c

    lax.fori_loop(0, n - 1, work, 0)
    recv[n - 1] = compute(me)

    def arrive(k, c):
        copy(k).wait()
        return c

    lax.fori_loop(0, n - 1, arrive, 0)

    def over(j, carry):
        color, s = carry
        piece = recv[lax.rem(me - j - 1 + 2 * n, n)].astype(jnp.float32)
        t = jnp.exp2(s)
        color = tuple(color[c] + t * piece[c * rb:(c + 1) * rb] for c in range(3))
        return color, s + piece[3 * rb:]

    init = jnp.zeros((rb, cols), jnp.float32)
    color, s = lax.fori_loop(0, n, over, ((init,) * 3, init))
    for c in range(3):
        out[c] = color[c]
    out[3] = one_minus_exp(s * -LN2)


def on_device(volume, tf_index, tf_table):
    depth, rows, cols = volume.shape
    n = lax.axis_size("depth")
    m = lax.axis_size("col")
    vm = pl.BlockSpec(memory_space=pltpu.VMEM)
    rb = rows // n
    return pl.pallas_call(
        functools.partial(kernel, n, m),
        out_shape=jax.ShapeDtypeStruct((4, rb, cols), jnp.float32),
        in_specs=[vm] * 3,
        out_specs=vm,
        scratch_shapes=[
            pltpu.VMEM((depth + 2, rows + 2 * PAD, cols), jnp.float32),
            pltpu.VMEM((depth, rows, cols), jnp.float32),
            pltpu.VMEM((n, 4 * rb, cols), jnp.bfloat16),
            pltpu.VMEM((n, 4 * rb, cols), jnp.bfloat16),
            *[pltpu.VMEM((rows, cols), jnp.bfloat16)] * 5,
            pltpu.SemaphoreType.DMA((n - 1,)),
            pltpu.SemaphoreType.DMA((n - 1,)),
            pltpu.SemaphoreType.DMA((4,)),
            pltpu.SemaphoreType.DMA((4,)),
        ],
        compiler_params=pltpu.CompilerParams(
            collective_id=0, has_side_effects=True, vmem_limit_bytes=32 * 1024 * 1024),
    )(volume, tf_index, tf_table)


def solution(mesh):
    in_specs = (P("depth", None, "col"), P("depth", None, "col"), P())
    out_specs = P(None, "depth", "col")
    return jax.shard_map(
        on_device, mesh=mesh, in_specs=in_specs, out_specs=out_specs, check_vma=False
    )
```

```python
import functools

import jax
import jax.numpy as jnp
from jax import lax
from jax.experimental import pallas as pl
from jax.experimental.pallas import tpu as pltpu
from jax.sharding import PartitionSpec as P

LIGHT = (0.75 * 0.36, 0.75 * 0.48, 0.75 * 0.8)
LOG2E = 1.4426950408889634
LN2 = 0.6931471805599453
PAD = 8


def one_minus_exp(x):
    series = x * (1.0 - x * (0.5 - x * (1.0 / 6.0 - x * (1.0 / 24.0 - x * (1.0 / 120.0)))))
    return jnp.where(x < 0.125, series, 1.0 - jnp.exp(-x))


def kernel(n, m, vol_hbm, idx_hbm, table_hbm, out, vol, idx, table, load_sem, fvol, dx, part, recv, edge, zlo, zhi, from_left, from_right,
           send_sem, recv_sem, halo_send, halo_recv):
    depth, rows, cols = vol.shape
    rb = rows // n
    me = lax.axis_index("depth")
    mine = lax.axis_index("col")

    loads = [pltpu.make_async_copy(src, dst, load_sem.at[i]) for i, (src, dst) in
             enumerate(((table_hbm, table), (vol_hbm, vol), (idx_hbm, idx)))]
    for load in loads:
        load.start()

    barrier = pltpu.get_barrier_semaphore()

    def greet(k, c):
        pl.semaphore_signal(barrier, inc=1, device_id={"depth": lax.rem(me + 1 + k, n)},
                            device_id_type=pl.DeviceIdType.MESH)
        return c

    lax.fori_loop(0, n - 1, greet, 0)
    for there, side in ((mine > 0, -1), (mine < m - 1, 1)):
        @pl.when(there)
        def _():
            pl.semaphore_signal(barrier, inc=1, device_id={"col": mine + side},
                                device_id_type=pl.DeviceIdType.MESH)

    def halo_copy(k, src, dst, axis, to):
        return pltpu.make_async_remote_copy(
            src_ref=src, dst_ref=dst, send_sem=halo_send.at[k], recv_sem=halo_recv.at[k],
            device_id={axis: to}, device_id_type=pl.DeviceIdType.MESH)

    along_z = ((me > 0, me < n - 1, halo_copy(0, vol.at[0], zhi, "depth", me - 1), zhi),
               (me < n - 1, me > 0, halo_copy(1, vol.at[depth - 1], zlo, "depth", me + 1), zlo))
    along_x = ((mine > 0, mine < m - 1, halo_copy(2, edge, from_right, "col", mine - 1), from_right),
               (mine < m - 1, mine > 0, halo_copy(3, edge, from_left, "col", mine + 1), from_left))

    def send(halos):
        for sends, _, copy, _ in halos:
            pl.when(sends)(copy.start)

    def receive(halos):
        for sends, receives, copy, landed in halos:
            pl.when(sends)(copy.wait_send)
            pl.when(receives)(copy.wait_recv)

            @pl.when(jnp.logical_not(receives))
            def _():
                landed[...] = jnp.zeros_like(landed)

    loads[0].wait()
    entries = table[...].astype(jnp.float32)
    sigma = entries[3:4]
    alpha = one_minus_exp(sigma)
    logs = [jnp.log(jnp.maximum(v, 1.2e-38)) * LOG2E
            for v in [entries[c:c + 1] * alpha for c in range(3)] + [sigma * LOG2E]]
    most = [jnp.max(v, axis=1, keepdims=True) for v in logs]
    least = [jnp.min(v, axis=1, keepdims=True) for v in logs]
    middle = [0.5 * (a + b) for a, b in zip(most, least)]
    grain = [jnp.maximum(a - b, 1e-3) * (1.0 / 65532.0) for a, b in zip(most, least)]
    place = [(v - o) / g for v, o, g in zip(logs, middle, grain)]

    def word(upper, lower):
        lower = jnp.floor(lower + 0.5)
        upper = jnp.floor(upper - lower * (1.0 / 65536.0) + 0.5)
        return upper.astype(jnp.int32) * 65536 + lower.astype(jnp.int32)

    sub = 8
    words = (word(place[0], place[1]), word(place[2], place[3]))
    low = [jnp.broadcast_to(t[:, :128], (sub, 128)) for t in words]
    high = [jnp.broadcast_to(t[:, 128:], (sub, 128)) for t in words]
    spread = [jnp.broadcast_to(g * (1.0 / 65536.0), (sub, cols)) for g in grain]
    sigma_middle = jnp.broadcast_to(middle[3], (sub, cols))
    scale = [jnp.broadcast_to(jnp.exp2(o), (sub, cols)) for o in middle[:3]]

    loads[1].wait()
    r_i = lax.broadcasted_iota(jnp.int32, (cols, cols), 0)
    c_i = lax.broadcasted_iota(jnp.int32, (cols, cols), 1)
    diff = jnp.where(r_i == c_i + 1, 1.0, 0.0) - jnp.where(r_i == c_i - 1, 1.0, 0.0)
    diff = diff.astype(jnp.bfloat16)
    zero = jnp.zeros((PAD, cols), jnp.float32)

    def pick(z, total):
        at = jnp.where((r_i == cols - 1) & (c_i == z), 1.0, 0.0)
        at = at + jnp.where((r_i == 0) & (c_i == depth + z), 1.0, 0.0)
        return total + jnp.dot(vol[z], at.astype(jnp.bfloat16), preferred_element_type=jnp.float32)

    edges = lax.fori_loop(0, depth, pick, jnp.zeros((rows, cols), jnp.float32), unroll=4)
    edge[...] = edges.astype(jnp.bfloat16)
    neighbours = (mine > 0).astype(jnp.int32) + (mine < m - 1).astype(jnp.int32)
    pl.semaphore_wait(barrier, n - 1 + neighbours)
    send(along_z)

    send(along_x)

    def widen(z, c):
        v = vol[z]
        fvol[z + 1, :PAD] = zero
        fvol[z + 1, PAD + rows:] = zero
        fvol[z + 1, PAD:PAD + rows] = v.astype(jnp.float32)
        return c

    lax.fori_loop(0, depth, widen, 0, unroll=2)
    receive(along_x)
    lane = lax.broadcasted_iota(jnp.int32, (rows, cols), 1)
    halo = jnp.where(lane < depth, from_left[...].astype(jnp.float32), from_right[...].astype(jnp.float32))
    halo = halo.astype(jnp.bfloat16)

    def stage(z, c):
        v = vol[z]
        ends = jnp.where((c_i == cols - 1) & (r_i == depth + z), 1.0, 0.0)
        ends = ends - jnp.where((c_i == 0) & (r_i == z), 1.0, 0.0)
        weights = jnp.concatenate([diff, ends.astype(jnp.bfloat16)], 0)
        both = jnp.concatenate([v, halo], 1)
        dx[z] = jnp.dot(both, weights, preferred_element_type=jnp.float32)
        return c

    lax.fori_loop(0, depth, stage, 0, unroll=4)
    receive(along_z)
    loads[2].wait()
    fvol[0, PAD:PAD + rows] = zlo[...].astype(jnp.float32)
    fvol[depth + 1, PAD:PAD + rows] = zhi[...].astype(jnp.float32)

    def block(r0):
        def step(z, carry):
            acc0, acc1, acc2, s = carry
            at = pl.multiple_of(PAD + r0, 8)
            gx = dx[z, pl.ds(pl.multiple_of(r0, 8), sub)]
            gy = fvol[z + 1, pl.ds(at + 1, sub)] - fvol[z + 1, pl.ds(at - 1, sub)]
            gz = fvol[z + 2, pl.ds(at, sub)] - fvol[z, pl.ds(at, sub)]
            facing = gx * LIGHT[0] + gy * LIGHT[1] + gz * LIGHT[2]
            inv = lax.rsqrt(gx * gx + gy * gy + (gz * gz + 4.0))
            shade = 0.25 + jnp.abs(facing) * inv
            label = idx[z, pl.ds(pl.multiple_of(r0, 8), sub)]
            in_low = label < 128
            lane = label & 127
            first, second = [jnp.where(in_low, jnp.take_along_axis(lo, lane, axis=1),
                                       jnp.take_along_axis(hi, lane, axis=1))
                             for lo, hi in zip(low, high)]
            codes = (first, first << 16, second, second << 16)
            code0, code1, code2, code3 = [c.astype(jnp.float32) * g for c, g in zip(codes, spread)]
            return (acc0 + jnp.exp2(code0 + s) * shade, acc1 + jnp.exp2(code1 + s) * shade,
                    acc2 + jnp.exp2(code2 + s) * shade, s - jnp.exp2(code3 + sigma_middle))

        init = tuple(jnp.zeros((sub, cols), jnp.float32) for _ in range(4))
        sums = lax.fori_loop(0, depth, step, init, unroll=True)
        return tuple(a * g for a, g in zip(sums[:3], scale)) + sums[3:]

    def compute(d):
        tiles = [block(d * rb + sub * i) for i in range(rb // sub)]
        return jnp.concatenate([t[c] for c in range(4) for t in tiles], 0).astype(jnp.bfloat16)

    def copy(k):
        return pltpu.make_async_remote_copy(
            src_ref=part.at[k], dst_ref=recv.at[k],
            send_sem=send_sem.at[k], recv_sem=recv_sem.at[k],
            device_id={"depth": lax.rem(me + 1 + k, n)},
            device_id_type=pl.DeviceIdType.MESH)

    def work(k, c):
        part[k] = compute(lax.rem(me + 1 + k, n))
        copy(k).start()
        return c

    lax.fori_loop(0, n - 1, work, 0)
    recv[n - 1] = compute(me)

    def arrive(k, c):
        copy(k).wait()
        return c

    lax.fori_loop(0, n - 1, arrive, 0)

    def over(j, carry):
        color, s = carry
        piece = recv[lax.rem(me - j - 1 + 2 * n, n)].astype(jnp.float32)
        t = jnp.exp2(s)
        color = tuple(color[c] + t * piece[c * rb:(c + 1) * rb] for c in range(3))
        return color, s + piece[3 * rb:]

    init = jnp.zeros((rb, cols), jnp.float32)
    color, s = lax.fori_loop(0, n, over, ((init,) * 3, init))
    for c in range(3):
        out[c] = color[c]
    out[3] = one_minus_exp(s * -LN2)


def on_device(volume, tf_index, tf_table):
    depth, rows, cols = volume.shape
    n = lax.axis_size("depth")
    m = lax.axis_size("col")
    vm = pl.BlockSpec(memory_space=pltpu.VMEM)
    rb = rows // n
    return pl.pallas_call(
        functools.partial(kernel, n, m),
        out_shape=jax.ShapeDtypeStruct((4, rb, cols), jnp.float32),
        in_specs=[pl.BlockSpec(memory_space=pltpu.HBM)] * 3,
        out_specs=vm,
        scratch_shapes=[
            pltpu.VMEM(volume.shape, volume.dtype),
            pltpu.VMEM(tf_index.shape, tf_index.dtype),
            pltpu.VMEM(tf_table.shape, tf_table.dtype),
            pltpu.SemaphoreType.DMA((3,)),
            pltpu.VMEM((depth + 2, rows + 2 * PAD, cols), jnp.float32),
            pltpu.VMEM((depth, rows, cols), jnp.float32),
            pltpu.VMEM((n, 4 * rb, cols), jnp.bfloat16),
            pltpu.VMEM((n, 4 * rb, cols), jnp.bfloat16),
            *[pltpu.VMEM((rows, cols), jnp.bfloat16)] * 5,
            pltpu.SemaphoreType.DMA((n - 1,)),
            pltpu.SemaphoreType.DMA((n - 1,)),
            pltpu.SemaphoreType.DMA((4,)),
            pltpu.SemaphoreType.DMA((4,)),
        ],
        compiler_params=pltpu.CompilerParams(
            collective_id=0, has_side_effects=True, vmem_limit_bytes=32 * 1024 * 1024),
    )(volume, tf_index, tf_table)


def solution(mesh):
    in_specs = (P("depth", None, "col"), P("depth", None, "col"), P())
    out_specs = P(None, "depth", "col")
    return jax.shard_map(
        on_device, mesh=mesh, in_specs=in_specs, out_specs=out_specs, check_vma=False
    )
```

```python
import functools

import jax
import jax.numpy as jnp
from jax import lax
from jax.experimental import pallas as pl
from jax.experimental.pallas import tpu as pltpu
from jax.sharding import PartitionSpec as P

LIGHT = (0.75 * 0.36, 0.75 * 0.48, 0.75 * 0.8)
LOG2E = 1.4426950408889634
LN2 = 0.6931471805599453
PAD = 8


def one_minus_exp(x):
    series = x * (1.0 - x * (0.5 - x * (1.0 / 6.0 - x * (1.0 / 24.0 - x * (1.0 / 120.0)))))
    return jnp.where(x < 0.125, series, 1.0 - jnp.exp(-x))


def kernel(n, m, vol_hbm, idx_hbm, table_hbm, out, vol, idx, table, load_sem, pre, fvol, dx, part, recv, edge, zlo, zhi, from_left, from_right,
           send_sem, recv_sem, halo_send, halo_recv):
    depth, rows, cols = vol.shape
    rb = rows // n
    me = lax.axis_index("depth")
    mine = lax.axis_index("col")

    loads = [pltpu.make_async_copy(src, dst, load_sem.at[i]) for i, (src, dst) in
             enumerate(((table_hbm, table), (vol_hbm, vol), (idx_hbm, idx)))]
    for load in loads:
        load.start()

    barrier = pltpu.get_barrier_semaphore()

    def greet(k, c):
        pl.semaphore_signal(barrier, inc=1, device_id={"depth": lax.rem(me + 1 + k, n)},
                            device_id_type=pl.DeviceIdType.MESH)
        return c

    lax.fori_loop(0, n - 1, greet, 0)
    for there, side in ((mine > 0, -1), (mine < m - 1, 1)):
        @pl.when(there)
        def _():
            pl.semaphore_signal(barrier, inc=1, device_id={"col": mine + side},
                                device_id_type=pl.DeviceIdType.MESH)

    def halo_copy(k, src, dst, axis, to):
        return pltpu.make_async_remote_copy(
            src_ref=src, dst_ref=dst, send_sem=halo_send.at[k], recv_sem=halo_recv.at[k],
            device_id={axis: to}, device_id_type=pl.DeviceIdType.MESH)

    along_z = ((me > 0, me < n - 1, halo_copy(0, vol.at[0], zhi, "depth", me - 1), zhi),
               (me < n - 1, me > 0, halo_copy(1, vol.at[depth - 1], zlo, "depth", me + 1), zlo))
    along_x = ((mine > 0, mine < m - 1, halo_copy(2, edge, from_right, "col", mine - 1), from_right),
               (mine < m - 1, mine > 0, halo_copy(3, edge, from_left, "col", mine + 1), from_left))

    def send(halos):
        for sends, _, copy, _ in halos:
            pl.when(sends)(copy.start)

    def receive(halos):
        for sends, receives, copy, landed in halos:
            pl.when(sends)(copy.wait_send)
            pl.when(receives)(copy.wait_recv)

            @pl.when(jnp.logical_not(receives))
            def _():
                landed[...] = jnp.zeros_like(landed)

    loads[0].wait()
    entries = table[...].astype(jnp.float32)
    sigma = entries[3:4]
    alpha = one_minus_exp(sigma)
    logs = [jnp.log(jnp.maximum(v, 1.2e-38)) * LOG2E
            for v in [entries[c:c + 1] * alpha for c in range(3)] + [sigma * LOG2E]]
    most = [jnp.max(v, axis=1, keepdims=True) for v in logs]
    least = [jnp.min(v, axis=1, keepdims=True) for v in logs]
    middle = [0.5 * (a + b) for a, b in zip(most, least)]
    grain = [jnp.maximum(a - b, 1e-3) * (1.0 / 65532.0) for a, b in zip(most, least)]
    place = [(v - o) / g for v, o, g in zip(logs, middle, grain)]

    def word(upper, lower):
        lower = jnp.floor(lower + 0.5)
        upper = jnp.floor(upper - lower * (1.0 / 65536.0) + 0.5)
        return upper.astype(jnp.int32) * 65536 + lower.astype(jnp.int32)

    sub = 8
    words = (word(place[0], place[1]), word(place[2], place[3]))
    low = [jnp.broadcast_to(t[:, :128], (sub, 128)) for t in words]
    high = [jnp.broadcast_to(t[:, 128:], (sub, 128)) for t in words]
    spread = [jnp.broadcast_to(g * (1.0 / 65536.0), (sub, cols)) for g in grain]
    sigma_middle = jnp.broadcast_to(middle[3], (sub, cols))
    scale = [jnp.broadcast_to(jnp.exp2(o), (sub, cols)) for o in middle[:3]]

    loads[1].wait()
    r_i = lax.broadcasted_iota(jnp.int32, (cols, cols), 0)
    c_i = lax.broadcasted_iota(jnp.int32, (cols, cols), 1)
    diff = jnp.where(r_i == c_i + 1, 1.0, 0.0) - jnp.where(r_i == c_i - 1, 1.0, 0.0)
    diff = diff.astype(jnp.bfloat16)
    zero = jnp.zeros((PAD, cols), jnp.float32)

    def pick(z, total):
        at = jnp.where((r_i == cols - 1) & (c_i == z), 1.0, 0.0)
        at = at + jnp.where((r_i == 0) & (c_i == depth + z), 1.0, 0.0)
        return total + jnp.dot(vol[z], at.astype(jnp.bfloat16), preferred_element_type=jnp.float32)

    edges = lax.fori_loop(0, depth, pick, jnp.zeros((rows, cols), jnp.float32), unroll=True)
    edge[...] = edges.astype(jnp.bfloat16)
    neighbours = (mine > 0).astype(jnp.int32) + (mine < m - 1).astype(jnp.int32)
    pl.semaphore_wait(barrier, n - 1 + neighbours)
    send(along_z)

    send(along_x)

    def search(word, z, r0):
        label = idx[z, pl.ds(r0, sub)]
        lane = label & 127
        return jnp.where(label < 128, jnp.take_along_axis(low[word], lane, axis=1),
                         jnp.take_along_axis(high[word], lane, axis=1))

    loads[2].wait()

    def widen(z, c):
        def rows_of(i, c):
            r0 = pl.multiple_of(i * sub, sub)
            pre[z, pl.ds(r0, sub)] = search(0, z, r0)
            return c

        lax.fori_loop(0, rows // sub, rows_of, 0, unroll=True)
        v = vol[z]
        fvol[z + 1, :PAD] = zero
        fvol[z + 1, PAD + rows:] = zero
        fvol[z + 1, PAD:PAD + rows] = v.astype(jnp.float32)
        return c

    lax.fori_loop(0, depth, widen, 0)
    receive(along_x)
    lane = lax.broadcasted_iota(jnp.int32, (rows, cols), 1)
    halo = jnp.where(lane < depth, from_left[...].astype(jnp.float32), from_right[...].astype(jnp.float32))
    halo = halo.astype(jnp.bfloat16)

    def stage(z, c):
        v = vol[z]
        ends = jnp.where((c_i == cols - 1) & (r_i == depth + z), 1.0, 0.0)
        ends = ends - jnp.where((c_i == 0) & (r_i == z), 1.0, 0.0)
        weights = jnp.concatenate([diff, ends.astype(jnp.bfloat16)], 0)
        both = jnp.concatenate([v, halo], 1)
        dx[z] = jnp.dot(both, weights, preferred_element_type=jnp.float32)
        return c

    lax.fori_loop(0, depth, stage, 0, unroll=8)
    receive(along_z)
    fvol[0, PAD:PAD + rows] = zlo[...].astype(jnp.float32)
    fvol[depth + 1, PAD:PAD + rows] = zhi[...].astype(jnp.float32)

    def block(r0):
        def step(z, carry):
            acc0, acc1, acc2, s = carry
            at = pl.multiple_of(PAD + r0, 8)
            gx = dx[z, pl.ds(pl.multiple_of(r0, 8), sub)]
            gy = fvol[z + 1, pl.ds(at + 1, sub)] - fvol[z + 1, pl.ds(at - 1, sub)]
            gz = fvol[z + 2, pl.ds(at, sub)] - fvol[z, pl.ds(at, sub)]
            facing = gx * LIGHT[0] + gy * LIGHT[1] + gz * LIGHT[2]
            inv = lax.rsqrt(gx * gx + gy * gy + (gz * gz + 4.0))
            shade = 0.25 + jnp.abs(facing) * inv
            r1 = pl.multiple_of(r0, 8)
            first, second = pre[z, pl.ds(r1, sub)], search(1, z, r1)
            codes = (first, first << 16, second, second << 16)
            code0, code1, code2, code3 = [c.astype(jnp.float32) * g for c, g in zip(codes, spread)]
            return (acc0 + jnp.exp2(code0 + s) * shade, acc1 + jnp.exp2(code1 + s) * shade,
                    acc2 + jnp.exp2(code2 + s) * shade, s - jnp.exp2(code3 + sigma_middle))

        init = tuple(jnp.zeros((sub, cols), jnp.float32) for _ in range(4))
        sums = lax.fori_loop(0, depth, step, init, unroll=True)
        return tuple(a * g for a, g in zip(sums[:3], scale)) + sums[3:]

    def compute(d):
        tiles = [block(d * rb + sub * i) for i in range(rb // sub)]
        return jnp.concatenate([t[c] for c in range(4) for t in tiles], 0).astype(jnp.bfloat16)

    def copy(k):
        return pltpu.make_async_remote_copy(
            src_ref=part.at[k], dst_ref=recv.at[k],
            send_sem=send_sem.at[k], recv_sem=recv_sem.at[k],
            device_id={"depth": lax.rem(me + 1 + k, n)},
            device_id_type=pl.DeviceIdType.MESH)

    def work(k, c):
        part[k] = compute(lax.rem(me + 1 + k, n))
        copy(k).start()
        return c

    lax.fori_loop(0, n - 1, work, 0)
    recv[n - 1] = compute(me)

    def arrive(k, c):
        copy(k).wait()
        return c

    lax.fori_loop(0, n - 1, arrive, 0)

    def over(j, carry):
        color, s = carry
        piece = recv[lax.rem(me - j - 1 + 2 * n, n)].astype(jnp.float32)
        t = jnp.exp2(s)
        color = tuple(color[c] + t * piece[c * rb:(c + 1) * rb] for c in range(3))
        return color, s + piece[3 * rb:]

    init = jnp.zeros((rb, cols), jnp.float32)
    color, s = lax.fori_loop(0, n, over, ((init,) * 3, init))
    for c in range(3):
        out[c] = color[c]
    out[3] = one_minus_exp(s * -LN2)


def on_device(volume, tf_index, tf_table):
    depth, rows, cols = volume.shape
    n = lax.axis_size("depth")
    m = lax.axis_size("col")
    vm = pl.BlockSpec(memory_space=pltpu.VMEM)
    rb = rows // n
    return pl.pallas_call(
        functools.partial(kernel, n, m),
        out_shape=jax.ShapeDtypeStruct((4, rb, cols), jnp.float32),
        in_specs=[pl.BlockSpec(memory_space=pltpu.HBM)] * 3,
        out_specs=vm,
        scratch_shapes=[
            pltpu.VMEM(volume.shape, volume.dtype),
            pltpu.VMEM(tf_index.shape, tf_index.dtype),
            pltpu.VMEM(tf_table.shape, tf_table.dtype),
            pltpu.SemaphoreType.DMA((3,)),
            pltpu.VMEM(tf_index.shape, jnp.int32),
            pltpu.VMEM((depth + 2, rows + 2 * PAD, cols), jnp.float32),
            pltpu.VMEM((depth, rows, cols), jnp.float32),
            pltpu.VMEM((n, 4 * rb, cols), jnp.bfloat16),
            pltpu.VMEM((n, 4 * rb, cols), jnp.bfloat16),
            *[pltpu.VMEM((rows, cols), jnp.bfloat16)] * 5,
            pltpu.SemaphoreType.DMA((n - 1,)),
            pltpu.SemaphoreType.DMA((n - 1,)),
            pltpu.SemaphoreType.DMA((4,)),
            pltpu.SemaphoreType.DMA((4,)),
        ],
        compiler_params=pltpu.CompilerParams(
            collective_id=0, has_side_effects=True, vmem_limit_bytes=62 * 1024 * 1024),
    )(volume, tf_index, tf_table)


def solution(mesh):
    in_specs = (P("depth", None, "col"), P("depth", None, "col"), P())
    out_specs = P(None, "depth", "col")
    return jax.shard_map(
        on_device, mesh=mesh, in_specs=in_specs, out_specs=out_specs, check_vma=False
    )
```

```python
import functools

import jax
import jax.numpy as jnp
from jax import lax
from jax.experimental import pallas as pl
from jax.experimental.pallas import tpu as pltpu
from jax.sharding import PartitionSpec as P

LIGHT = (0.75 * 0.36, 0.75 * 0.48, 0.75 * 0.8)
LOG2E = 1.4426950408889634
LN2 = 0.6931471805599453
PAD = 8


def one_minus_exp(x):
    series = x * (1.0 - x * (0.5 - x * (1.0 / 6.0 - x * (1.0 / 24.0 - x * (1.0 / 120.0)))))
    return jnp.where(x < 0.125, series, 1.0 - jnp.exp(-x))


def kernel(n, m, vol_hbm, idx_hbm, table_hbm, out, vol, idx, table, load_sem, pre, fvol, dx, part, recv, edge, zlo, zhi, from_left, from_right,
           send_sem, recv_sem, halo_send, halo_recv):
    depth, rows, cols = vol.shape
    rb = rows // n
    me = lax.axis_index("depth")
    mine = lax.axis_index("col")

    loads = [pltpu.make_async_copy(src, dst, load_sem.at[i]) for i, (src, dst) in
             enumerate(((table_hbm, table), (vol_hbm, vol), (idx_hbm, idx)))]
    for load in loads:
        load.start()

    barrier = pltpu.get_barrier_semaphore()

    def greet(k, c):
        pl.semaphore_signal(barrier, inc=1, device_id={"depth": lax.rem(me + 1 + k, n)},
                            device_id_type=pl.DeviceIdType.MESH)
        return c

    lax.fori_loop(0, n - 1, greet, 0)
    for there, side in ((mine > 0, -1), (mine < m - 1, 1)):
        @pl.when(there)
        def _():
            pl.semaphore_signal(barrier, inc=1, device_id={"col": mine + side},
                                device_id_type=pl.DeviceIdType.MESH)

    def halo_copy(k, src, dst, axis, to):
        return pltpu.make_async_remote_copy(
            src_ref=src, dst_ref=dst, send_sem=halo_send.at[k], recv_sem=halo_recv.at[k],
            device_id={axis: to}, device_id_type=pl.DeviceIdType.MESH)

    along_z = ((me > 0, me < n - 1, halo_copy(0, vol.at[0], zhi, "depth", me - 1), zhi),
               (me < n - 1, me > 0, halo_copy(1, vol.at[depth - 1], zlo, "depth", me + 1), zlo))
    along_x = ((mine > 0, mine < m - 1, halo_copy(2, edge, from_right, "col", mine - 1), from_right),
               (mine < m - 1, mine > 0, halo_copy(3, edge, from_left, "col", mine + 1), from_left))

    def send(halos):
        for sends, _, copy, _ in halos:
            pl.when(sends)(copy.start)

    def receive(halos):
        for sends, receives, copy, landed in halos:
            pl.when(sends)(copy.wait_send)
            pl.when(receives)(copy.wait_recv)

            @pl.when(jnp.logical_not(receives))
            def _():
                landed[...] = jnp.zeros_like(landed)

    loads[0].wait()
    entries = table[...].astype(jnp.float32)
    sigma = entries[3:4]
    alpha = one_minus_exp(sigma)
    logs = [jnp.log(jnp.maximum(v, 1.2e-38)) * LOG2E
            for v in [entries[c:c + 1] * alpha for c in range(3)] + [sigma * LOG2E]]
    most = [jnp.max(v, axis=1, keepdims=True) for v in logs]
    least = [jnp.min(v, axis=1, keepdims=True) for v in logs]
    middle = [0.5 * (a + b) for a, b in zip(most, least)]
    grain = [jnp.maximum(a - b, 1e-3) * (1.0 / 65532.0) for a, b in zip(most, least)]
    place = [(v - o) / g for v, o, g in zip(logs, middle, grain)]

    def word(upper, lower):
        lower = jnp.floor(lower + 0.5)
        upper = jnp.floor(upper - lower * (1.0 / 65536.0) + 0.5)
        return upper.astype(jnp.int32) * 65536 + lower.astype(jnp.int32)

    sub = 8
    words = (word(place[0], place[1]), word(place[2], place[3]))
    low = [jnp.broadcast_to(t[:, :128], (sub, 128)) for t in words]
    high = [jnp.broadcast_to(t[:, 128:], (sub, 128)) for t in words]
    spread = [jnp.broadcast_to(g * (1.0 / 65536.0), (sub, cols)) for g in grain]
    sigma_middle = jnp.broadcast_to(middle[3], (sub, cols))
    scale = [jnp.broadcast_to(jnp.exp2(o), (sub, cols)) for o in middle[:3]]

    loads[1].wait()
    r_i = lax.broadcasted_iota(jnp.int32, (cols, cols), 0)
    c_i = lax.broadcasted_iota(jnp.int32, (cols, cols), 1)
    diff = jnp.where(r_i == c_i + 1, 1.0, 0.0) - jnp.where(r_i == c_i - 1, 1.0, 0.0)
    diff = diff.astype(jnp.bfloat16)
    zero = jnp.zeros((PAD, cols), jnp.float32)

    def pick(z, total):
        at = jnp.where((r_i == cols - 1) & (c_i == z), 1.0, 0.0)
        at = at + jnp.where((r_i == 0) & (c_i == depth + z), 1.0, 0.0)
        return total + jnp.dot(vol[z], at.astype(jnp.bfloat16), preferred_element_type=jnp.float32)

    edges = lax.fori_loop(0, depth, pick, jnp.zeros((rows, cols), jnp.float32), unroll=True)
    fold = cols // (2 * depth)
    short = rows // fold
    packed = edges[:short]
    for i in range(1, fold):
        packed = packed + pltpu.roll(edges[i * short:(i + 1) * short], 2 * depth * i, 1)
    edge[...] = packed.astype(jnp.bfloat16)
    neighbours = (mine > 0).astype(jnp.int32) + (mine < m - 1).astype(jnp.int32)
    pl.semaphore_wait(barrier, n - 1 + neighbours)
    send(along_z)

    send(along_x)

    def search(word, z, r0):
        label = idx[z, pl.ds(r0, sub)]
        lane = label & 127
        return jnp.where(label < 128, jnp.take_along_axis(low[word], lane, axis=1),
                         jnp.take_along_axis(high[word], lane, axis=1))

    loads[2].wait()

    early = depth * 12 // 16

    def widen(z, c):
        def rows_of(i, c):
            r0 = pl.multiple_of(i * sub, sub)
            pre[z, pl.ds(r0, sub)] = search(0, z, r0)
            return c

        @pl.when(z < early)
        def _():
            lax.fori_loop(0, rows // sub, rows_of, 0, unroll=True)

        v = vol[z]
        fvol[z + 1, :PAD] = zero
        fvol[z + 1, PAD + rows:] = zero
        fvol[z + 1, PAD:PAD + rows] = v.astype(jnp.float32)
        return c

    lax.fori_loop(0, depth, widen, 0)
    receive(along_x)
    lane = lax.broadcasted_iota(jnp.int32, (short, cols), 1)
    packed = jnp.where(lax.rem(lane, 2 * depth) < depth, from_left[...].astype(jnp.float32),
                       from_right[...].astype(jnp.float32))
    halo = [packed] + [pltpu.roll(packed, cols - 2 * depth * i, 1) for i in range(1, fold)]
    halo = jnp.concatenate(halo, 0).astype(jnp.bfloat16)

    def stage(z, c):
        v = vol[z]
        ends = jnp.where((c_i == cols - 1) & (r_i == depth + z), 1.0, 0.0)
        ends = ends - jnp.where((c_i == 0) & (r_i == z), 1.0, 0.0)
        weights = jnp.concatenate([diff, ends.astype(jnp.bfloat16)], 0)
        both = jnp.concatenate([v, halo], 1)
        dx[z] = jnp.dot(both, weights, preferred_element_type=jnp.float32)
        return c

    lax.fori_loop(0, depth, stage, 0, unroll=8)
    receive(along_z)
    fvol[0, PAD:PAD + rows] = zlo[...].astype(jnp.float32)
    fvol[depth + 1, PAD:PAD + rows] = zhi[...].astype(jnp.float32)

    def block(r0):
        def step(z, carry, known):
            acc0, acc1, acc2, s = carry
            at = pl.multiple_of(PAD + r0, 8)
            gx = dx[z, pl.ds(pl.multiple_of(r0, 8), sub)]
            gy = fvol[z + 1, pl.ds(at + 1, sub)] - fvol[z + 1, pl.ds(at - 1, sub)]
            gz = fvol[z + 2, pl.ds(at, sub)] - fvol[z, pl.ds(at, sub)]
            facing = gx * LIGHT[0] + gy * LIGHT[1] + gz * LIGHT[2]
            inv = lax.rsqrt(gx * gx + gy * gy + (gz * gz + 4.0))
            shade = 0.25 + jnp.abs(facing) * inv
            r1 = pl.multiple_of(r0, 8)
            first = pre[z, pl.ds(r1, sub)] if known else search(0, z, r1)
            second = search(1, z, r1)
            codes = (first, first << 16, second, second << 16)
            code0, code1, code2, code3 = [c.astype(jnp.float32) * g for c, g in zip(codes, spread)]
            return (acc0 + jnp.exp2(code0 + s) * shade, acc1 + jnp.exp2(code1 + s) * shade,
                    acc2 + jnp.exp2(code2 + s) * shade, s - jnp.exp2(code3 + sigma_middle))

        init = tuple(jnp.zeros((sub, cols), jnp.float32) for _ in range(4))
        sums = lax.fori_loop(0, early, functools.partial(step, known=True), init, unroll=True)
        sums = lax.fori_loop(early, depth, functools.partial(step, known=False), sums, unroll=True)
        return tuple(a * g for a, g in zip(sums[:3], scale)) + sums[3:]

    def compute(d):
        tiles = [block(d * rb + sub * i) for i in range(rb // sub)]
        return jnp.concatenate([t[c] for c in range(4) for t in tiles], 0).astype(jnp.bfloat16)

    def copy(k):
        return pltpu.make_async_remote_copy(
            src_ref=part.at[k], dst_ref=recv.at[k],
            send_sem=send_sem.at[k], recv_sem=recv_sem.at[k],
            device_id={"depth": lax.rem(me + 1 + k, n)},
            device_id_type=pl.DeviceIdType.MESH)

    def work(k, c):
        part[k] = compute(lax.rem(me + 1 + k, n))
        copy(k).start()
        return c

    lax.fori_loop(0, n - 1, work, 0)
    recv[n - 1] = compute(me)

    def arrive(k, c):
        copy(k).wait()
        return c

    lax.fori_loop(0, n - 1, arrive, 0)

    def over(j, carry):
        color, s = carry
        piece = recv[lax.rem(me - j - 1 + 2 * n, n)].astype(jnp.float32)
        t = jnp.exp2(s)
        color = tuple(color[c] + t * piece[c * rb:(c + 1) * rb] for c in range(3))
        return color, s + piece[3 * rb:]

    init = jnp.zeros((rb, cols), jnp.float32)
    color, s = lax.fori_loop(0, n, over, ((init,) * 3, init))
    for c in range(3):
        out[c] = color[c]
    out[3] = one_minus_exp(s * -LN2)


def on_device(volume, tf_index, tf_table):
    depth, rows, cols = volume.shape
    n = lax.axis_size("depth")
    m = lax.axis_size("col")
    vm = pl.BlockSpec(memory_space=pltpu.VMEM)
    rb = rows // n
    return pl.pallas_call(
        functools.partial(kernel, n, m),
        out_shape=jax.ShapeDtypeStruct((4, rb, cols), jnp.float32),
        in_specs=[pl.BlockSpec(memory_space=pltpu.HBM)] * 3,
        out_specs=vm,
        scratch_shapes=[
            pltpu.VMEM(volume.shape, volume.dtype),
            pltpu.VMEM(tf_index.shape, tf_index.dtype),
            pltpu.VMEM(tf_table.shape, tf_table.dtype),
            pltpu.SemaphoreType.DMA((3,)),
            pltpu.VMEM(tf_index.shape, jnp.int32),
            pltpu.VMEM((depth + 2, rows + 2 * PAD, cols), jnp.float32),
            pltpu.VMEM((depth, rows, cols), jnp.float32),
            pltpu.VMEM((n, 4 * rb, cols), jnp.bfloat16),
            pltpu.VMEM((n, 4 * rb, cols), jnp.bfloat16),
            pltpu.VMEM((2 * rows * depth // cols, cols), jnp.bfloat16),
            *[pltpu.VMEM((rows, cols), jnp.bfloat16)] * 2,
            *[pltpu.VMEM((2 * rows * depth // cols, cols), jnp.bfloat16)] * 2,
            pltpu.SemaphoreType.DMA((n - 1,)),
            pltpu.SemaphoreType.DMA((n - 1,)),
            pltpu.SemaphoreType.DMA((4,)),
            pltpu.SemaphoreType.DMA((4,)),
        ],
        compiler_params=pltpu.CompilerParams(
            collective_id=0, has_side_effects=True, vmem_limit_bytes=62 * 1024 * 1024),
    )(volume, tf_index, tf_table)


def solution(mesh):
    in_specs = (P("depth", None, "col"), P("depth", None, "col"), P())
    out_specs = P(None, "depth", "col")
    return jax.shard_map(
        on_device, mesh=mesh, in_specs=in_specs, out_specs=out_specs, check_vma=False
    )
```

```python
import functools

import jax
import jax.numpy as jnp
from jax import lax
from jax.experimental import pallas as pl
from jax.experimental.pallas import tpu as pltpu
from jax.sharding import PartitionSpec as P

LIGHT = (0.75 * 0.36, 0.75 * 0.48, 0.75 * 0.8)
LOG2E = 1.4426950408889634
LN2 = 0.6931471805599453
PAD = 8


def one_minus_exp(x):
    series = x * (1.0 - x * (0.5 - x * (1.0 / 6.0 - x * (1.0 / 24.0 - x * (1.0 / 120.0)))))
    return jnp.where(x < 0.125, series, 1.0 - jnp.exp(-x))


def kernel(n, m, vol_hbm, idx_hbm, table_hbm, out, vol, idx, table, load_sem, pre, fvol, dx, part, recv, edge, zlo, zhi, from_left, from_right,
           send_sem, recv_sem, halo_send, halo_recv):
    depth, rows, cols = vol.shape
    rb = rows // n
    me = lax.axis_index("depth")
    mine = lax.axis_index("col")

    loads = [pltpu.make_async_copy(src, dst, load_sem.at[i]) for i, (src, dst) in
             enumerate(((table_hbm, table), (vol_hbm, vol), (idx_hbm, idx)))]
    for load in loads:
        load.start()

    barrier = pltpu.get_barrier_semaphore()

    def greet(k, c):
        pl.semaphore_signal(barrier, inc=1, device_id={"depth": lax.rem(me + 1 + k, n)},
                            device_id_type=pl.DeviceIdType.MESH)
        return c

    lax.fori_loop(0, n - 1, greet, 0)
    for there, side in ((mine > 0, -1), (mine < m - 1, 1)):
        @pl.when(there)
        def _():
            pl.semaphore_signal(barrier, inc=1, device_id={"col": mine + side},
                                device_id_type=pl.DeviceIdType.MESH)

    def halo_copy(k, src, dst, axis, to):
        return pltpu.make_async_remote_copy(
            src_ref=src, dst_ref=dst, send_sem=halo_send.at[k], recv_sem=halo_recv.at[k],
            device_id={axis: to}, device_id_type=pl.DeviceIdType.MESH)

    along_z = ((me > 0, me < n - 1, halo_copy(0, vol.at[0], zhi, "depth", me - 1), zhi),
               (me < n - 1, me > 0, halo_copy(1, vol.at[depth - 1], zlo, "depth", me + 1), zlo))
    along_x = ((mine > 0, mine < m - 1, halo_copy(2, edge, from_right, "col", mine - 1), from_right),
               (mine < m - 1, mine > 0, halo_copy(3, edge, from_left, "col", mine + 1), from_left))

    def send(halos):
        for sends, _, copy, _ in halos:
            pl.when(sends)(copy.start)

    def receive(halos):
        for sends, receives, copy, landed in halos:
            pl.when(sends)(copy.wait_send)
            pl.when(receives)(copy.wait_recv)

            @pl.when(jnp.logical_not(receives))
            def _():
                landed[...] = jnp.zeros_like(landed)

    loads[1].wait()
    r_i = lax.broadcasted_iota(jnp.int32, (cols, cols), 0)
    c_i = lax.broadcasted_iota(jnp.int32, (cols, cols), 1)
    diff = jnp.where(r_i == c_i + 1, 1.0, 0.0) - jnp.where(r_i == c_i - 1, 1.0, 0.0)
    diff = diff.astype(jnp.bfloat16)
    zero = jnp.zeros((PAD, cols), jnp.float32)

    def pick(z, total):
        at = jnp.where((r_i == cols - 1) & (c_i == z), 1.0, 0.0)
        at = at + jnp.where((r_i == 0) & (c_i == depth + z), 1.0, 0.0)
        return total + jnp.dot(vol[z], at.astype(jnp.bfloat16), preferred_element_type=jnp.float32)

    edges = lax.fori_loop(0, depth, pick, jnp.zeros((rows, cols), jnp.float32), unroll=True)
    fold = cols // (2 * depth)
    short = rows // fold
    packed = edges[:short]
    for i in range(1, fold):
        packed = packed + pltpu.roll(edges[i * short:(i + 1) * short], 2 * depth * i, 1)
    edge[...] = packed.astype(jnp.bfloat16)
    neighbours = (mine > 0).astype(jnp.int32) + (mine < m - 1).astype(jnp.int32)
    pl.semaphore_wait(barrier, n - 1 + neighbours)
    send(along_z)

    send(along_x)

    loads[0].wait()
    entries = table[...].astype(jnp.float32)
    sigma = entries[3:4]
    alpha = one_minus_exp(sigma)
    logs = [jnp.log(jnp.maximum(v, 1.2e-38)) * LOG2E
            for v in [entries[c:c + 1] * alpha for c in range(3)] + [sigma * LOG2E]]
    most = [jnp.max(v, axis=1, keepdims=True) for v in logs]
    least = [jnp.min(v, axis=1, keepdims=True) for v in logs]
    middle = [0.5 * (a + b) for a, b in zip(most, least)]
    grain = [jnp.maximum(a - b, 1e-3) * (1.0 / 65532.0) for a, b in zip(most, least)]
    place = [(v - o) / g for v, o, g in zip(logs, middle, grain)]

    def word(upper, lower):
        lower = jnp.floor(lower + 0.5)
        upper = jnp.floor(upper - lower * (1.0 / 65536.0) + 0.5)
        return upper.astype(jnp.int32) * 65536 + lower.astype(jnp.int32)

    sub = 8
    words = (word(place[0], place[1]), word(place[2], place[3]))
    low = [jnp.broadcast_to(t[:, :128], (sub, 128)) for t in words]
    high = [jnp.broadcast_to(t[:, 128:], (sub, 128)) for t in words]
    spread = [jnp.broadcast_to(g * (1.0 / 65536.0), (sub, cols)) for g in grain]
    sigma_middle = jnp.broadcast_to(middle[3], (sub, cols))
    scale = [jnp.broadcast_to(jnp.exp2(o), (sub, cols)) for o in middle[:3]]

    def search(word, z, r0):
        label = idx[z, pl.ds(r0, sub)]
        lane = label & 127
        return jnp.where(label < 128, jnp.take_along_axis(low[word], lane, axis=1),
                         jnp.take_along_axis(high[word], lane, axis=1))

    loads[2].wait()

    early = depth * 12 // 16

    def widen(z, c):
        def rows_of(i, c):
            r0 = pl.multiple_of(i * sub, sub)
            pre[z, pl.ds(r0, sub)] = search(0, z, r0)
            return c

        @pl.when(z < early)
        def _():
            lax.fori_loop(0, rows // sub, rows_of, 0, unroll=True)

        v = vol[z]
        fvol[z + 1, :PAD] = zero
        fvol[z + 1, PAD + rows:] = zero
        fvol[z + 1, PAD:PAD + rows] = v.astype(jnp.float32)
        return c

    lax.fori_loop(0, depth, widen, 0)
    receive(along_x)
    lane = lax.broadcasted_iota(jnp.int32, (short, cols), 1)
    packed = jnp.where(lax.rem(lane, 2 * depth) < depth, from_left[...].astype(jnp.float32),
                       from_right[...].astype(jnp.float32))
    halo = [packed] + [pltpu.roll(packed, cols - 2 * depth * i, 1) for i in range(1, fold)]
    halo = jnp.concatenate(halo, 0).astype(jnp.bfloat16)

    def stage(z, c):
        v = vol[z]
        ends = jnp.where((c_i == cols - 1) & (r_i == depth + z), 1.0, 0.0)
        ends = ends - jnp.where((c_i == 0) & (r_i == z), 1.0, 0.0)
        weights = jnp.concatenate([diff, ends.astype(jnp.bfloat16)], 0)
        both = jnp.concatenate([v, halo], 1)
        dx[z] = jnp.dot(both, weights, preferred_element_type=jnp.float32)
        return c

    lax.fori_loop(0, depth, stage, 0, unroll=8)
    receive(along_z)
    fvol[0, PAD:PAD + rows] = zlo[...].astype(jnp.float32)
    fvol[depth + 1, PAD:PAD + rows] = zhi[...].astype(jnp.float32)

    def block(r0):
        def step(z, carry, known):
            acc0, acc1, acc2, s = carry
            at = pl.multiple_of(PAD + r0, 8)
            gx = dx[z, pl.ds(pl.multiple_of(r0, 8), sub)]
            gy = fvol[z + 1, pl.ds(at + 1, sub)] - fvol[z + 1, pl.ds(at - 1, sub)]
            gz = fvol[z + 2, pl.ds(at, sub)] - fvol[z, pl.ds(at, sub)]
            facing = gx * LIGHT[0] + gy * LIGHT[1] + gz * LIGHT[2]
            inv = lax.rsqrt(gx * gx + gy * gy + (gz * gz + 4.0))
            shade = 0.25 + jnp.abs(facing) * inv
            r1 = pl.multiple_of(r0, 8)
            first = pre[z, pl.ds(r1, sub)] if known else search(0, z, r1)
            second = search(1, z, r1)
            codes = (first, first << 16, second, second << 16)
            code0, code1, code2, code3 = [c.astype(jnp.float32) * g for c, g in zip(codes, spread)]
            return (acc0 + jnp.exp2(code0 + s) * shade, acc1 + jnp.exp2(code1 + s) * shade,
                    acc2 + jnp.exp2(code2 + s) * shade, s - jnp.exp2(code3 + sigma_middle))

        init = tuple(jnp.zeros((sub, cols), jnp.float32) for _ in range(4))
        sums = lax.fori_loop(0, early, functools.partial(step, known=True), init, unroll=True)
        sums = lax.fori_loop(early, depth, functools.partial(step, known=False), sums, unroll=True)
        return tuple(a * g for a, g in zip(sums[:3], scale)) + sums[3:]

    def compute(d):
        tiles = [block(d * rb + sub * i) for i in range(rb // sub)]
        return jnp.concatenate([t[c] for c in range(4) for t in tiles], 0).astype(jnp.bfloat16)

    def copy(k):
        return pltpu.make_async_remote_copy(
            src_ref=part.at[k], dst_ref=recv.at[k],
            send_sem=send_sem.at[k], recv_sem=recv_sem.at[k],
            device_id={"depth": lax.rem(me + 1 + k, n)},
            device_id_type=pl.DeviceIdType.MESH)

    def work(k, c):
        part[k] = compute(lax.rem(me + 1 + k, n))
        copy(k).start()
        return c

    lax.fori_loop(0, n - 1, work, 0)
    recv[n - 1] = compute(me)

    def arrive(k, c):
        copy(k).wait()
        return c

    lax.fori_loop(0, n - 1, arrive, 0)

    def over(j, carry):
        color, s = carry
        piece = recv[lax.rem(me - j - 1 + 2 * n, n)].astype(jnp.float32)
        t = jnp.exp2(s)
        color = tuple(color[c] + t * piece[c * rb:(c + 1) * rb] for c in range(3))
        return color, s + piece[3 * rb:]

    init = jnp.zeros((rb, cols), jnp.float32)
    color, s = lax.fori_loop(0, n, over, ((init,) * 3, init))
    for c in range(3):
        out[c] = color[c]
    out[3] = one_minus_exp(s * -LN2)


def on_device(volume, tf_index, tf_table):
    depth, rows, cols = volume.shape
    n = lax.axis_size("depth")
    m = lax.axis_size("col")
    vm = pl.BlockSpec(memory_space=pltpu.VMEM)
    rb = rows // n
    return pl.pallas_call(
        functools.partial(kernel, n, m),
        out_shape=jax.ShapeDtypeStruct((4, rb, cols), jnp.float32),
        in_specs=[pl.BlockSpec(memory_space=pltpu.HBM)] * 3,
        out_specs=vm,
        scratch_shapes=[
            pltpu.VMEM(volume.shape, volume.dtype),
            pltpu.VMEM(tf_index.shape, tf_index.dtype),
            pltpu.VMEM(tf_table.shape, tf_table.dtype),
            pltpu.SemaphoreType.DMA((3,)),
            pltpu.VMEM(tf_index.shape, jnp.int32),
            pltpu.VMEM((depth + 2, rows + 2 * PAD, cols), jnp.float32),
            pltpu.VMEM((depth, rows, cols), jnp.float32),
            pltpu.VMEM((n, 4 * rb, cols), jnp.bfloat16),
            pltpu.VMEM((n, 4 * rb, cols), jnp.bfloat16),
            pltpu.VMEM((2 * rows * depth // cols, cols), jnp.bfloat16),
            *[pltpu.VMEM((rows, cols), jnp.bfloat16)] * 2,
            *[pltpu.VMEM((2 * rows * depth // cols, cols), jnp.bfloat16)] * 2,
            pltpu.SemaphoreType.DMA((n - 1,)),
            pltpu.SemaphoreType.DMA((n - 1,)),
            pltpu.SemaphoreType.DMA((4,)),
            pltpu.SemaphoreType.DMA((4,)),
        ],
        compiler_params=pltpu.CompilerParams(
            collective_id=0, has_side_effects=True, vmem_limit_bytes=62 * 1024 * 1024),
    )(volume, tf_index, tf_table)


def solution(mesh):
    in_specs = (P("depth", None, "col"), P("depth", None, "col"), P())
    out_specs = P(None, "depth", "col")
    return jax.shard_map(
        on_device, mesh=mesh, in_specs=in_specs, out_specs=out_specs, check_vma=False
    )
```
